32 devices in a mesh: src: 8 (over z, y), sta: 4 (over x, core).
Axes of the slice: x: 2, y: 2, z: 4, core: 2. Of those that a mesh axis runs over, the one named last changes fastest.
Arguments:
- trace: float32 [256, 8256], P('sta', 'src'), may hold values from -6 to 6
- quadrature: float32 [256, 8256], P('sta', 'src'), may hold values from -6 to 6
- gains: float32 [256], P('sta'), may hold values from 0.3 to 3
- lags: int32 [1024, 256], P('src', 'sta'), may hold values from 0 to 63
Outputs:
- beam_power: float32 [2, 1024], P(None, 'src')
The draws below stay inside these ranges and needn't reach their ends.
All inputs are finite; a program needn't handle non-finite values.
Results may differ from the reference program's by a relative error of at most 0.0003.
Values may be sent and summed in bfloat16 or wider, within the bound.
A program may use at most 256 MiB of HBM per device.

```python
import math
import jax
import jax.numpy as jnp
from jax import lax

W = 4096
LAGS = 64
STEPS = 2
NT = 8256
S = 256
C = 1024


def set_ends(values, stream_key, low, top_value):
    extent = values.shape
    index_at = [jax.random.randint(jax.random.fold_in(stream_key, axis), (), 0, extent[axis]) for axis in range(len(extent))]
    values = values.at[tuple(index_at)].set(low)
    longest = extent.index(max(extent))
    index_at[longest] = (index_at[longest] + 1) % extent[longest]
    return values.at[tuple(index_at)].set(top_value)


def steps_of(rng, shape, split, low, largest):
    level, own = 1.0, jax.random.fold_in(rng, 6)
    for dim, blocks in split:
        heights = jnp.exp(jax.random.uniform(jax.random.fold_in(own, dim), (blocks,), jnp.float32, low / len(split), largest / len(split)))
        level = level * jnp.repeat(heights, shape[dim] // blocks).reshape([-1 if axis == dim else 1 for axis in range(len(shape))])
    return level


def bell_draw(key, shape, deviation, limit, shards=(), held_as=jnp.bfloat16):
    values = jax.random.normal(key, shape, jnp.float32) * deviation
    if len(shards) > 0:
        values = steps_of(key, shape, shards, -0.22, 0.18) * values
    return jnp.clip(values, min=-limit, max=limit).astype(held_as)


def setup_inputs(seed: int = 0) -> dict:
    keys = jax.random.split(jax.random.key(seed), 5)
    trace = bell_draw(keys[0], (S, NT), 1.0, 6.0, ((0, 4), (1, 8)), jnp.float32)
    quadrature = bell_draw(keys[1], (S, NT), 1.0, 6.0, ((0, 4), (1, 8)), jnp.float32)
    gains = jnp.clip(jnp.exp(math.log(3.0) - 2.3025851 * jax.random.uniform(keys[2], (S,), jnp.float32) ** steps_of(keys[2], (S,), ((0, 4),), -0.2, 0.2)), 0.3, 3.0)
    lags = set_ends(jax.random.randint(keys[3], (C, S), 0, LAGS), jax.random.fold_in(keys[3], 1), 0, LAGS - 1).astype(jnp.int32)
    return dict(trace=trace, quadrature=quadrature, gains=gains, lags=lags)


def reference(trace, quadrature, gains, lags):
    energy = trace * trace + quadrature * quadrature
    baseline = jnp.mean(energy, axis=1, keepdims=True)
    weighted = (gains[:, None] * (energy - baseline)).astype(jnp.bfloat16)
    weighted_wide = weighted.astype(jnp.float32)
    cell_total = lags.shape[0]
    power_rows = []
    for step_index in range(STEPS):
        def add_lag(summed, lag_value):
            selector = (lags == lag_value).astype(jnp.float32)
            window = lax.dynamic_slice_in_dim(weighted_wide, (step_index * W + lag_value).astype(jnp.int32), W, 1)
            return summed + jnp.dot(selector, window, precision=lax.Precision.HIGHEST), None

        beam, unused = lax.scan(add_lag, jnp.zeros((cell_total, W), jnp.float32), jnp.arange(LAGS, dtype=jnp.int32))
        power_rows.append(jnp.sum(beam * beam, axis=1))
    power = jnp.stack(power_rows)
    return power / jnp.max(power, axis=1, keepdims=True)
```

```python
import functools

import jax
import jax.numpy as jnp
from jax import lax
from jax.experimental import pallas as pl
from jax.experimental.pallas import tpu as pltpu
from jax.sharding import PartitionSpec as P

W = 4096
LAGS = 64
STEPS = 2
SUB = 16
CORES = 2


def kernel(
    n_src, n_sta,
    trace_ref, quad_ref, gains_ref, lags_ref, out_ref,
    energy_t, edge_out, edge_in, stat, lag_all, lag_group, packed, wide, shifted, picks, acc, part, whole,
    stat_send, stat_recv, edge_send, edge_recv, lag_send, lag_recv, group_send, group_recv,
    pack_send, pack_recv, fwd_send, fwd_recv, part_send, part_recv, whole_send, whole_recv,
):
    i = lax.axis_index("src")
    j = lax.axis_index("sta")
    stations, block = trace_ref.shape
    cells = lags_ref.shape[0]
    span = STEPS * W // n_src
    rows = span + LAGS
    half = rows // 2
    per = n_src // n_sta
    chips = n_sta // CORES
    chip, core = j // CORES, j % CORES
    mate = chip * CORES + (1 - core)

    def remote(src, dst, send, recv, where):
        copy = pltpu.make_async_remote_copy(
            src_ref=src, dst_ref=dst, send_sem=send, recv_sem=recv,
            device_id=where, device_id_type=pl.DeviceIdType.MESH,
        )
        copy.start()
        return copy

    def src_at(d):
        return ((i + d) % n_src, j)

    def sta_at(d):
        return (i, (j + d) % n_sta)

    barrier = pltpu.get_barrier_semaphore()
    for d in range(1, n_src):
        pl.semaphore_signal(barrier, inc=1, device_id=src_at(d), device_id_type=pl.DeviceIdType.MESH)
    for d in range(1, n_sta):
        pl.semaphore_signal(barrier, inc=1, device_id=sta_at(d), device_id_type=pl.DeviceIdType.MESH)

    own = trace_ref[...] * trace_ref[...] + quad_ref[...] * quad_ref[...]
    own_t = own.T
    energy_t[LAGS : LAGS + block, :] = own_t
    edge_out[0] = own_t[:LAGS]
    edge_out[1] = own_t[block - LAGS :]
    stat[0] = jnp.sum(own_t, axis=0, keepdims=True)
    lag_all[i] = lags_ref[...].astype(jnp.float32).T.astype(jnp.bfloat16)
    pl.semaphore_wait(barrier, n_src + n_sta - 2)

    stat_copies = [remote(stat.at[0], stat.at[d], stat_send.at[d], stat_recv.at[d], src_at(d)) for d in range(1, n_src)]
    edge_copies = [
        remote(edge_out.at[0], edge_in.at[1], edge_send.at[0], edge_recv.at[1], src_at(n_src - 1)),
        remote(edge_out.at[1], edge_in.at[0], edge_send.at[1], edge_recv.at[0], src_at(1)),
    ]
    lag_copies = [remote(lag_all.at[i], lag_all.at[i], lag_send.at[d], lag_recv.at[d], src_at(d)) for d in range(1, n_src)]

    for copy in stat_copies + edge_copies:
        copy.wait_recv()
    baseline = jnp.sum(stat[...], axis=0) / (block * n_src)
    energy_t[0:LAGS, :] = edge_in[0]
    energy_t[LAGS + block :, :] = edge_in[1]
    offset = LAGS - (LAGS // n_src) * i
    upper = gains_ref[...] * (energy_t[pl.ds(offset, half), :] - baseline)
    lower = gains_ref[...] * (energy_t[pl.ds(offset + half, half), :] - baseline)
    packed[j] = jnp.concatenate([upper, lower], axis=1).astype(jnp.bfloat16)

    pack_copies = [remote(packed.at[j], packed.at[j], pack_send.at[0], pack_recv.at[0], (i, mate))]
    for c in range(1, chips):
        there = (j + c * CORES) % n_sta
        pack_copies.append(remote(packed.at[j], packed.at[j], pack_send.at[c], pack_recv.at[c], (i, there)))

    for copy in lag_copies:
        copy.wait_recv()
    group_copies = []
    for d in range(1, n_sta):
        there = (j + d) % n_sta
        group_copies.append(remote(
            lag_all.at[pl.ds(there * per, per)], lag_group.at[j], group_send.at[d], group_recv.at[d], (i, there),
        ))
    lag_group[j] = lag_all[pl.ds(j * per, per)]

    pack_copies[0].wait_recv()
    for copy in group_copies:
        copy.wait_recv()

    low_lanes = lax.broadcasted_iota(jnp.int32, (half, 2 * stations), 1) < stations
    acc[...] = jnp.zeros_like(acc)
    copied = span + LAGS - SUB
    for phase in range(chips):
        first = ((chip + phase) % chips) * CORES
        if phase >= 1:
            source = (j + (chips - phase) * CORES) % n_sta
            fwd_copies[phase - 1].wait_recv()
        a = packed[first].astype(jnp.float32)
        b = packed[first + 1].astype(jnp.float32)
        wide[0:half, :] = jnp.where(low_lanes, a, pltpu.roll(b, stations, 1))
        wide[half:rows, :] = jnp.where(low_lanes, pltpu.roll(a, stations, 1), b)
        for s in range(SUB):
            shifted[s] = wide[s : s + copied, :].astype(jnp.bfloat16)
        lag_pair = jnp.concatenate(
            [jnp.concatenate([lag_group[first + c, q] for q in range(per)], axis=1) for c in range(CORES)], axis=0
        )
        if phase == 0:
            fwd_copies = []
            for c in range(1, chips):
                pack_copies[c].wait_recv()
                source = (j + (chips - c) * CORES) % n_sta
                fwd_copies.append(remote(
                    packed.at[source], packed.at[source], fwd_send.at[c], fwd_recv.at[c], (i, mate),
                ))

        def add_lags(coarse, carry):
            start = pl.multiple_of(coarse * SUB, SUB)
            for s in range(SUB):
                lag = (start + s).astype(jnp.float32).astype(jnp.bfloat16)
                picks[s * 2 * stations : (s + 1) * 2 * stations, :] = jnp.where(
                    lag_pair == lag, jnp.bfloat16(1), jnp.bfloat16(0)
                )
            left = jnp.concatenate([shifted[s, pl.ds(start, span), :] for s in range(SUB)], axis=1)
            acc[...] += jnp.dot(left, picks[...], preferred_element_type=jnp.float32)
            return carry

        lax.fori_loop(0, LAGS // SUB, add_lags, 0)

    part[i] = jnp.sum(acc[...] * acc[...], axis=0, keepdims=True)
    part_copies = [remote(part.at[i], part.at[i], part_send.at[d], part_recv.at[d], src_at(d)) for d in range(1, n_src)]
    for copy in part_copies:
        copy.wait_recv()
    share = n_src // STEPS
    whole[j] = jnp.concatenate(
        [jnp.sum(part[k * share : (k + 1) * share], axis=0) for k in range(STEPS)], axis=0
    )
    whole_copies = [remote(whole.at[j], whole.at[j], whole_send.at[d], whole_recv.at[d], sta_at(d)) for d in range(1, n_sta)]
    for copy in whole_copies:
        copy.wait_recv()
    peak = jnp.max(jnp.max(whole[...], axis=0), axis=1, keepdims=True)
    mine = whole[i // per]
    place = i % per
    result = mine[:, :cells]
    for q in range(1, per):
        result = jnp.where(place == q, mine[:, q * cells : (q + 1) * cells], result)
    out_ref[...] = result / peak
    for copy in stat_copies + edge_copies + lag_copies + pack_copies + group_copies + fwd_copies + part_copies + whole_copies:
        copy.wait_send()


def on_device(n_src, n_sta, trace, quadrature, gains, lags):
    stations, block = trace.shape
    cells = lags.shape[0]
    per = n_src // n_sta
    chips = n_sta // CORES
    span = STEPS * W // n_src
    rows = span + LAGS
    dma = pltpu.SemaphoreType.DMA
    return pl.pallas_call(
        functools.partial(kernel, n_src, n_sta),
        out_shape=jax.ShapeDtypeStruct((STEPS, cells), jnp.float32),
        in_specs=[pl.BlockSpec(memory_space=pltpu.VMEM)] * 4,
        out_specs=pl.BlockSpec(memory_space=pltpu.VMEM),
        scratch_shapes=[
            pltpu.VMEM((block + 2 * LAGS, stations), jnp.float32),
            pltpu.VMEM((2, LAGS, stations), jnp.float32),
            pltpu.VMEM((2, LAGS, stations), jnp.float32),
            pltpu.VMEM((n_src, 1, stations), jnp.float32),
            pltpu.VMEM((n_src, stations, cells), jnp.bfloat16),
            pltpu.VMEM((n_sta, per, stations, cells), jnp.bfloat16),
            pltpu.VMEM((n_sta, rows // 2, 2 * stations), jnp.bfloat16),
            pltpu.VMEM((rows, 2 * stations), jnp.float32),
            pltpu.VMEM((SUB, rows - SUB, 2 * stations), jnp.bfloat16),
            pltpu.VMEM((SUB * 2 * stations, per * cells), jnp.bfloat16),
            pltpu.VMEM((span, per * cells), jnp.float32),
            pltpu.VMEM((n_src, 1, per * cells), jnp.float32),
            pltpu.VMEM((n_sta, STEPS, per * cells), jnp.float32),
            dma((n_src,)), dma((n_src,)),
            dma((2,)), dma((2,)),
            dma((n_src,)), dma((n_src,)),
            dma((n_sta,)), dma((n_sta,)),
            dma((chips,)), dma((chips,)),
            dma((chips,)), dma((chips,)),
            dma((n_src,)), dma((n_src,)),
            dma((n_sta,)), dma((n_sta,)),
        ],
        compiler_params=pltpu.CompilerParams(
            collective_id=0, has_side_effects=True, vmem_limit_bytes=48 * 1024 * 1024
        ),
    )(trace, quadrature, gains.reshape(1, stations), lags)


def solution(mesh):
    return jax.shard_map(
        functools.partial(on_device, mesh.shape["src"], mesh.shape["sta"]),
        mesh=mesh,
        in_specs=(P("sta", "src"), P("sta", "src"), P("sta"), P("src", "sta")),
        out_specs=P(None, "src"),
        check_vma=False,
    )
```

```python
import functools

import jax
import jax.numpy as jnp
from jax import lax
from jax.experimental import pallas as pl
from jax.experimental.pallas import tpu as pltpu
from jax.sharding import PartitionSpec as P

W = 4096
LAGS = 64
STEPS = 2
SUB = 16
CORES = 2


def kernel(
    n_src, n_sta,
    trace_hbm, quad_hbm, gains_ref, lags_hbm, out_ref,
    trace_ref, quad_ref, lags_ref, energy_t, edge_out, edge_in, total, lag_out, lag_group, packed, wide, shifted, picks, acc, part,
    load_sem, total_send, total_recv, edge_send, edge_recv, lag_send, lag_recv, pack_send, pack_recv, fwd_send, fwd_recv,
    part_send, part_recv,
):
    i = lax.axis_index("src")
    j = lax.axis_index("sta")
    stations, block = trace_ref.shape
    cells = lags_ref.shape[1]
    span = STEPS * W // n_src
    rows = span + LAGS
    half = rows // 2
    per = n_src // n_sta
    chips = n_sta // CORES
    everyone = n_src * n_sta
    chip, core = j // CORES, j % CORES
    mate = chip * CORES + (1 - core)

    def remote(src, dst, send, recv, where):
        return pltpu.make_async_remote_copy(
            src_ref=src, dst_ref=dst, send_sem=send, recv_sem=recv,
            device_id=where, device_id_type=pl.DeviceIdType.MESH,
        )

    def peer(d):
        return ((i + d // n_sta) % n_src, (j + d % n_sta) % n_sta)

    loads = [
        pltpu.make_async_copy(trace_hbm, trace_ref, load_sem.at[0]),
        pltpu.make_async_copy(quad_hbm, quad_ref, load_sem.at[1]),
        pltpu.make_async_copy(lags_hbm, lags_ref, load_sem.at[2]),
    ]
    for load in loads:
        load.start()
    barrier = pltpu.get_barrier_semaphore()

    def greet(d, carry):
        pl.semaphore_signal(barrier, inc=1, device_id=peer(d), device_id_type=pl.DeviceIdType.MESH)
        return carry

    lax.fori_loop(1, everyone, greet, 0)
    for load in loads:
        load.wait()

    lag_out[...] = lags_ref[...].astype(jnp.float32).astype(jnp.bfloat16)
    own_t = (trace_ref[...] * trace_ref[...] + quad_ref[...] * quad_ref[...]).T * gains_ref[...]
    energy_t[LAGS : LAGS + block, :] = own_t
    edge_out[0] = own_t[:LAGS]
    edge_out[1] = own_t[block - LAGS :]
    own_total = jnp.sum(own_t, axis=0, keepdims=True)
    total[i, j] = own_total
    own_mean = own_total / block
    offset = LAGS - (LAGS // n_src) * i
    upper = energy_t[pl.ds(offset, half), :] - own_mean
    lower = energy_t[pl.ds(offset + half, half), :] - own_mean
    packed[j] = jnp.concatenate([upper, lower], axis=1).astype(jnp.bfloat16)
    pl.semaphore_wait(barrier, everyone - 1)

    def total_copy(d):
        return remote(total.at[i, j], total.at[i, j], total_send.at[d], total_recv.at[d], peer(d))

    pack_copies = [remote(packed.at[j], packed.at[j], pack_send.at[0], pack_recv.at[0], (i, mate))]
    for c in range(1, chips):
        there = (j + c * CORES) % n_sta
        pack_copies.append(remote(packed.at[j], packed.at[j], pack_send.at[c], pack_recv.at[c], (i, there)))
    owner = i // per
    slot = i % per
    lag_copies = [
        remote(lag_out, lag_group.at[j, slot], lag_send.at[d], lag_recv.at[slot * n_sta + j], ((i + d) % n_src, owner))
        for d in range(n_src)
    ]
    edge_copies = []
    for d in range(n_sta):
        column = (j + d) % n_sta
        edge_copies.append(remote(
            edge_out.at[0], edge_in.at[1, j], edge_send.at[0, d], edge_recv.at[1, d], ((i + n_src - 1) % n_src, column)))
        edge_copies.append(remote(
            edge_out.at[1], edge_in.at[0, j], edge_send.at[1, d], edge_recv.at[0, d], ((i + 1) % n_src, column)))

    pack_copies[0].start()
    for copy in pack_copies[1:]:
        copy.start()
    for d in range(1, n_sta):
        total_copy(d).start()
    for copy in lag_copies[1:]:
        copy.start()

    @pl.when(owner != j)
    def _():
        lag_copies[0].start()

    @pl.when(owner == j)
    def _():
        lag_group[j, slot] = lag_out[...]

    for copy in edge_copies:
        copy.start()

    def send_total(d, carry):
        total_copy(d).start()
        return carry

    lax.fori_loop(n_sta, everyone, send_total, 0)

    for d in range(1, n_sta):
        total_copy(d).wait_recv()
    pack_copies[0].wait_recv()
    for copy in edge_copies:
        copy.wait_recv()
    for q in range(per):
        for c in range(n_sta):
            landed = remote(
                lag_out, lag_group.at[c, q], lag_send.at[0], lag_recv.at[q * n_sta + c], (i, mate))

            @pl.when(jnp.logical_or(j * per + q != i, j != c))
            def _():
                landed.wait_recv()

    low_lanes = lax.broadcasted_iota(jnp.int32, (half, 2 * stations), 1) < stations
    acc[...] = jnp.zeros_like(acc)
    copied = span + LAGS - SUB
    fwd_copies = []
    for phase in range(chips):
        first = ((chip + phase) % chips) * CORES
        if phase >= 1:
            fwd_copies[phase - 1].wait_recv()
        a = packed[first].astype(jnp.float32)
        b = packed[first + 1].astype(jnp.float32)
        wide[pl.ds(offset, half), :] = jnp.where(low_lanes, a, pltpu.roll(b, stations, 1))
        wide[pl.ds(offset + half, half), :] = jnp.where(low_lanes, pltpu.roll(a, stations, 1), b)
        for side, start in ((0, 0), (1, LAGS + block)):
            wide[start : start + LAGS, :] = jnp.concatenate(
                [edge_in[side, first + c] - total[i, first + c] / block for c in range(CORES)], axis=1
            )
        for s in range(SUB):
            shifted[s] = wide[pl.ds(offset + s, copied), :].astype(jnp.bfloat16)
        lag_pair = jnp.concatenate(
            [jnp.concatenate([lag_group[first + c, q] for q in range(per)], axis=1) for c in range(CORES)], axis=0
        )
        if phase == 0:
            for c in range(1, chips):
                pack_copies[c].wait_recv()
                source = (j + (chips - c) * CORES) % n_sta
                fwd_copies.append(remote(
                    packed.at[source], packed.at[source], fwd_send.at[c], fwd_recv.at[c], (i, mate)))
                fwd_copies[-1].start()

        def add_lags(coarse, carry):
            start = pl.multiple_of(coarse * SUB, SUB)
            for s in range(SUB):
                lag = (start + s).astype(jnp.float32).astype(jnp.bfloat16)
                picks[s * 2 * stations : (s + 1) * 2 * stations, :] = jnp.where(
                    lag_pair == lag, jnp.bfloat16(1), jnp.bfloat16(0)
                )
            left = jnp.concatenate([shifted[s, pl.ds(start, span), :] for s in range(SUB)], axis=1)
            acc[...] += jnp.dot(left, picks[...], preferred_element_type=jnp.float32)
            return carry

        lax.fori_loop(0, LAGS // SUB, add_lags, 0)

    def take_total(d, carry):
        total_copy(d).wait_recv()
        return carry

    lax.fori_loop(n_sta, everyone, take_total, 0)

    def summed(x):
        return jnp.sum(jnp.sum(jnp.sum(x, axis=0), axis=0), axis=1, keepdims=True)

    shift = summed(total[...]) / (block * n_src) - summed(total[pl.ds(i, 1)]) / block
    beam = acc[...] - shift
    part[i, j] = jnp.sum(beam * beam, axis=0, keepdims=True)

    def part_copy(d):
        return remote(part.at[i, j], part.at[i, j], part_send.at[d], part_recv.at[d], peer(d))

    def send_part(d, carry):
        part_copy(d).start()
        return carry

    def take_part(d, carry):
        part_copy(d).wait_recv()
        return carry

    lax.fori_loop(1, everyone, send_part, 0)

    for copy in edge_copies + pack_copies + fwd_copies + lag_copies[1:]:
        copy.wait_send()

    @pl.when(owner != j)
    def _():
        lag_copies[0].wait_send()

    def sent(d, carry):
        total_copy(d).wait_send()
        return carry

    lax.fori_loop(1, everyone, sent, 0)
    lax.fori_loop(1, everyone, take_part, 0)

    share = n_src // STEPS
    place = i % per
    for k in range(STEPS):
        power = jnp.sum(part[k * share : (k + 1) * share], axis=0)
        peak = jnp.max(jnp.max(power, axis=0), axis=1, keepdims=True)
        mine = jnp.sum(part[k * share : (k + 1) * share, owner], axis=0)
        result = mine[:, :cells]
        for q in range(1, per):
            result = jnp.where(place == q, mine[:, q * cells : (q + 1) * cells], result)
        out_ref[k : k + 1, :] = result / peak

    def part_sent(d, carry):
        part_copy(d).wait_send()
        return carry

    lax.fori_loop(1, everyone, part_sent, 0)


def on_device(n_src, n_sta, trace, quadrature, gains, lags):
    stations, block = trace.shape
    cells = lags.shape[0]
    per = n_src // n_sta
    chips = n_sta // CORES
    span = STEPS * W // n_src
    rows = span + LAGS
    everyone = n_src * n_sta
    dma = pltpu.SemaphoreType.DMA
    hbm = pl.BlockSpec(memory_space=pltpu.HBM)
    return pl.pallas_call(
        functools.partial(kernel, n_src, n_sta),
        out_shape=jax.ShapeDtypeStruct((STEPS, cells), jnp.float32),
        in_specs=[hbm, hbm, pl.BlockSpec(memory_space=pltpu.VMEM), hbm],
        out_specs=pl.BlockSpec(memory_space=pltpu.VMEM),
        scratch_shapes=[
            pltpu.VMEM((stations, block), jnp.float32),
            pltpu.VMEM((stations, block), jnp.float32),
            pltpu.VMEM((stations, cells), jnp.int32),
            pltpu.VMEM((block + 2 * LAGS, stations), jnp.float32),
            pltpu.VMEM((2, LAGS, stations), jnp.float32),
            pltpu.VMEM((2, n_sta, LAGS, stations), jnp.float32),
            pltpu.VMEM((n_src, n_sta, 1, stations), jnp.float32),
            pltpu.VMEM((stations, cells), jnp.bfloat16),
            pltpu.VMEM((n_sta, per, stations, cells), jnp.bfloat16),
            pltpu.VMEM((n_sta, rows // 2, 2 * stations), jnp.bfloat16),
            pltpu.VMEM((block + 2 * LAGS, 2 * stations), jnp.float32),
            pltpu.VMEM((SUB, rows - SUB, 2 * stations), jnp.bfloat16),
            pltpu.VMEM((SUB * 2 * stations, per * cells), jnp.bfloat16),
            pltpu.VMEM((span, per * cells), jnp.float32),
            pltpu.VMEM((n_src, n_sta, 1, per * cells), jnp.float32),
            dma((3,)),
            dma((everyone,)), dma((everyone,)),
            dma((2, n_sta)), dma((2, n_sta)),
            dma((n_src,)), dma((n_src,)),
            dma((chips,)), dma((chips,)),
            dma((chips,)), dma((chips,)),
            dma((everyone,)), dma((everyone,)),
        ],
        compiler_params=pltpu.CompilerParams(
            collective_id=0, has_side_effects=True, vmem_limit_bytes=48 * 1024 * 1024
        ),
    )(trace, quadrature, gains.reshape(1, stations), lags.T)


def solution(mesh):
    return jax.shard_map(
        functools.partial(on_device, mesh.shape["src"], mesh.shape["sta"]),
        mesh=mesh,
        in_specs=(P("sta", "src"), P("sta", "src"), P("sta"), P("src", "sta")),
        out_specs=P(None, "src"),
        check_vma=False,
    )
```

```python
import functools

import jax
import jax.numpy as jnp
from jax import lax
from jax.experimental import pallas as pl
from jax.experimental.pallas import tpu as pltpu
from jax.sharding import PartitionSpec as P

W = 4096
LAGS = 64
STEPS = 2
SUB = 16
CORES = 2


def kernel(
    n_src, n_sta,
    trace_hbm, quad_hbm, gains_ref, lags_hbm, out_ref,
    trace_ref, quad_ref, lags_ref, energy_t, edge_out, edge_in, total, lag_out, lag_group, packed, wide, shifted, picks, acc, part,
    load_sem, total_send, total_recv, edge_send, edge_recv, lag_send, lag_recv, pack_send, pack_recv, fwd_send, fwd_recv,
    part_send, part_recv,
):
    i = lax.axis_index("src")
    j = lax.axis_index("sta")
    stations, block = trace_ref.shape
    cells = lags_ref.shape[1]
    span = STEPS * W // n_src
    rows = span + LAGS
    half = rows // 2
    per = n_src // n_sta
    chips = n_sta // CORES
    everyone = n_src * n_sta
    chip, core = j // CORES, j % CORES
    mate = chip * CORES + (1 - core)

    def remote(src, dst, send, recv, where):
        return pltpu.make_async_remote_copy(
            src_ref=src, dst_ref=dst, send_sem=send, recv_sem=recv,
            device_id=where, device_id_type=pl.DeviceIdType.MESH,
        )

    def wrap(x, n):
        return jnp.where(x >= n, x - n, x)

    def peer(d):
        return wrap(i + d // n_sta, n_src), wrap(j + d % n_sta, n_sta)

    def each(low, high, step):
        for d in range(low, high):
            step(d, 0)

    loads = [
        pltpu.make_async_copy(trace_hbm, trace_ref, load_sem.at[0]),
        pltpu.make_async_copy(quad_hbm, quad_ref, load_sem.at[1]),
        pltpu.make_async_copy(lags_hbm, lags_ref, load_sem.at[2]),
    ]
    for load in loads:
        load.start()
    barrier = pltpu.get_barrier_semaphore()

    def greet(d, carry):
        pl.semaphore_signal(barrier, inc=1, device_id=peer(d), device_id_type=pl.DeviceIdType.MESH)
        return carry

    each(1, everyone, greet)
    for load in loads:
        load.wait()

    lag_out[...] = lags_ref[...].astype(jnp.float32).astype(jnp.bfloat16)
    own_t = (trace_ref[...] * trace_ref[...] + quad_ref[...] * quad_ref[...]).T * gains_ref[...]
    energy_t[LAGS : LAGS + block, :] = own_t
    edge_out[0] = own_t[:LAGS]
    edge_out[1] = own_t[block - LAGS :]
    own_total = jnp.sum(own_t, axis=0, keepdims=True)
    total[i, j] = own_total
    own_mean = own_total / block
    offset = LAGS - (LAGS // n_src) * i
    upper = energy_t[pl.ds(offset, half), :] - own_mean
    lower = energy_t[pl.ds(offset + half, half), :] - own_mean
    packed[j] = jnp.concatenate([upper, lower], axis=1).astype(jnp.bfloat16)
    pl.semaphore_wait(barrier, everyone - 1)

    def total_copy(d):
        return remote(total.at[i, j], total.at[i, j], total_send.at[d], total_recv.at[d], peer(d))

    pack_copies = [remote(packed.at[j], packed.at[j], pack_send.at[0], pack_recv.at[0], (i, mate))]
    for c in range(1, chips):
        there = wrap(j + c * CORES, n_sta)
        pack_copies.append(remote(packed.at[j], packed.at[j], pack_send.at[c], pack_recv.at[c], (i, there)))
    owner = i // per
    slot = i % per
    lag_copies = [
        remote(lag_out, lag_group.at[j, slot], lag_send.at[d], lag_recv.at[slot * n_sta + j], (wrap(i + d, n_src), owner))
        for d in range(n_src)
    ]
    edge_copies = []
    for d, column in enumerate([j, mate] + [wrap(j + c * CORES, n_sta) for c in range(1, chips)] + [wrap(mate + c * CORES, n_sta) for c in range(1, chips)]):
        edge_copies.append(remote(
            edge_out.at[0], edge_in.at[1, j], edge_send.at[0, d], edge_recv.at[1, j], (wrap(i + n_src - 1, n_src), column)))
        edge_copies.append(remote(
            edge_out.at[1], edge_in.at[0, j], edge_send.at[1, d], edge_recv.at[0, j], (wrap(i + 1, n_src), column)))

    for d in range(1, n_sta):
        total_copy(d).start()
    pack_copies[0].start()
    for copy in lag_copies[1:]:
        copy.start()

    @pl.when(owner != j)
    def _():
        lag_copies[0].start()

    @pl.when(owner == j)
    def _():
        lag_group[j, slot] = lag_out[...]

    for copy in edge_copies[: 2 * CORES] + pack_copies[1:] + edge_copies[2 * CORES :]:
        copy.start()

    def send_total(d, carry):
        total_copy(d).start()
        return carry

    each(n_sta, everyone, send_total)

    for d in range(1, n_sta):
        total_copy(d).wait_recv()
    pack_copies[0].wait_recv()

    def take_column(c):
        for side in range(2):
            remote(edge_out.at[side], edge_in.at[side, c], edge_send.at[side, 0], edge_recv.at[side, c], (i, mate)).wait_recv()
        for q in range(per):
            landed = remote(lag_out, lag_group.at[c, q], lag_send.at[0], lag_recv.at[q * n_sta + c], (i, mate))

            @pl.when(jnp.logical_or(j * per + q != i, j != c))
            def _():
                landed.wait_recv()

    low_lanes = lax.broadcasted_iota(jnp.int32, (half, 2 * stations), 1) < stations
    acc[...] = jnp.zeros_like(acc)
    copied = span + LAGS - SUB
    fwd_copies = []
    for phase in range(chips):
        first = ((chip + phase) % chips) * CORES
        if phase >= 1:
            fwd_copies[phase - 1].wait_recv()
        for c in range(CORES):
            take_column(first + c)
        a = packed[first].astype(jnp.float32)
        b = packed[first + 1].astype(jnp.float32)
        wide[pl.ds(offset, half), :] = jnp.where(low_lanes, a, pltpu.roll(b, stations, 1))
        wide[pl.ds(offset + half, half), :] = jnp.where(low_lanes, pltpu.roll(a, stations, 1), b)
        for side, start in ((0, 0), (1, LAGS + block)):
            wide[start : start + LAGS, :] = jnp.concatenate(
                [edge_in[side, first + c] - total[i, first + c] / block for c in range(CORES)], axis=1
            )
        for s in range(SUB):
            shifted[s] = wide[pl.ds(offset + s, copied), :].astype(jnp.bfloat16)
        lag_pair = jnp.concatenate(
            [jnp.concatenate([lag_group[first + c, q] for q in range(per)], axis=1) for c in range(CORES)], axis=0
        )
        if phase == 0:
            for c in range(1, chips):
                source = wrap(j + (chips - c) * CORES, n_sta)
                fwd_copies.append(remote(
                    packed.at[source], packed.at[source], fwd_send.at[c], fwd_recv.at[c], (i, mate)))

        def add_lags(coarse, carry):
            start = pl.multiple_of(coarse * SUB, SUB)
            if phase == 0:

                @pl.when(coarse == LAGS // SUB - 1)
                def _():
                    for c in range(1, chips):
                        pack_copies[c].wait_recv()
                        fwd_copies[c - 1].start()

            for s in range(SUB):
                lag = (start + s).astype(jnp.float32).astype(jnp.bfloat16)
                picks[s * 2 * stations : (s + 1) * 2 * stations, :] = jnp.where(
                    lag_pair == lag, jnp.bfloat16(1), jnp.bfloat16(0)
                )
            left = jnp.concatenate([shifted[s, pl.ds(start, span), :] for s in range(SUB)], axis=1)
            acc[...] += jnp.dot(left, picks[...], preferred_element_type=jnp.float32)
            return carry

        lax.fori_loop(0, LAGS // SUB, add_lags, 0)

    def take_total(d, carry):
        total_copy(d).wait_recv()
        return carry

    each(n_sta, everyone, take_total)

    def summed(x):
        return jnp.sum(jnp.sum(jnp.sum(x, axis=0), axis=0), axis=1, keepdims=True)

    shift = summed(total[...]) / (block * n_src) - summed(total[pl.ds(i, 1)]) / block
    beam = acc[...] - shift
    part[i, j] = jnp.sum(beam * beam, axis=0, keepdims=True)

    def part_copy(d):
        return remote(part.at[i, j], part.at[i, j], part_send.at[d], part_recv.at[d], peer(d))

    def send_part(d, carry):
        part_copy(d).start()
        return carry

    def take_part(d, carry):
        part_copy(d).wait_recv()
        return carry

    each(1, everyone, send_part)

    for copy in edge_copies + pack_copies + fwd_copies + lag_copies[1:]:
        copy.wait_send()

    @pl.when(owner != j)
    def _():
        lag_copies[0].wait_send()

    def sent(d, carry):
        total_copy(d).wait_send()
        return carry

    each(1, everyone, sent)
    each(1, everyone, take_part)

    share = n_src // STEPS
    place = i % per
    for k in range(STEPS):
        power = jnp.sum(part[k * share : (k + 1) * share], axis=0)
        peak = jnp.max(jnp.max(power, axis=0), axis=1, keepdims=True)
        mine = jnp.sum(part[k * share : (k + 1) * share, owner], axis=0)
        result = mine[:, :cells]
        for q in range(1, per):
            result = jnp.where(place == q, mine[:, q * cells : (q + 1) * cells], result)
        out_ref[k : k + 1, :] = result / peak

    def part_sent(d, carry):
        part_copy(d).wait_send()
        return carry

    each(1, everyone, part_sent)


def on_device(n_src, n_sta, trace, quadrature, gains, lags):
    stations, block = trace.shape
    cells = lags.shape[0]
    per = n_src // n_sta
    chips = n_sta // CORES
    span = STEPS * W // n_src
    rows = span + LAGS
    everyone = n_src * n_sta
    dma = pltpu.SemaphoreType.DMA
    hbm = pl.BlockSpec(memory_space=pltpu.HBM)
    return pl.pallas_call(
        functools.partial(kernel, n_src, n_sta),
        out_shape=jax.ShapeDtypeStruct((STEPS, cells), jnp.float32),
        in_specs=[hbm, hbm, pl.BlockSpec(memory_space=pltpu.VMEM), hbm],
        out_specs=pl.BlockSpec(memory_space=pltpu.VMEM),
        scratch_shapes=[
            pltpu.VMEM((stations, block), jnp.float32),
            pltpu.VMEM((stations, block), jnp.float32),
            pltpu.VMEM((stations, cells), jnp.int32),
            pltpu.VMEM((block + 2 * LAGS, stations), jnp.float32),
            pltpu.VMEM((2, LAGS, stations), jnp.float32),
            pltpu.VMEM((2, n_sta, LAGS, stations), jnp.float32),
            pltpu.VMEM((n_src, n_sta, 1, stations), jnp.float32),
            pltpu.VMEM((stations, cells), jnp.bfloat16),
            pltpu.VMEM((n_sta, per, stations, cells), jnp.bfloat16),
            pltpu.VMEM((n_sta, rows // 2, 2 * stations), jnp.bfloat16),
            pltpu.VMEM((block + 2 * LAGS, 2 * stations), jnp.float32),
            pltpu.VMEM((SUB, rows - SUB, 2 * stations), jnp.bfloat16),
            pltpu.VMEM((SUB * 2 * stations, per * cells), jnp.bfloat16),
            pltpu.VMEM((span, per * cells), jnp.float32),
            pltpu.VMEM((n_src, n_sta, 1, per * cells), jnp.float32),
            dma((3,)),
            dma((everyone,)), dma((everyone,)),
            dma((2, n_sta)), dma((2, n_sta)),
            dma((n_src,)), dma((n_src,)),
            dma((chips,)), dma((chips,)),
            dma((chips,)), dma((chips,)),
            dma((everyone,)), dma((everyone,)),
        ],
        compiler_params=pltpu.CompilerParams(
            collective_id=0, has_side_effects=True, vmem_limit_bytes=62 * 1024 * 1024
        ),
    )(trace, quadrature, gains.reshape(1, stations), lags.T)


def solution(mesh):
    return jax.shard_map(
        functools.partial(on_device, mesh.shape["src"], mesh.shape["sta"]),
        mesh=mesh,
        in_specs=(P("sta", "src"), P("sta", "src"), P("sta"), P("src", "sta")),
        out_specs=P(None, "src"),
        check_vma=False,
    )
```

```python
import functools

import jax
import jax.numpy as jnp
from jax import lax
from jax.experimental import pallas as pl
from jax.experimental.pallas import tpu as pltpu
from jax.sharding import PartitionSpec as P

W = 4096
LAGS = 64
STEPS = 2
SUB = 16
CORES = 2


def kernel(
    n_src, n_sta,
    trace_hbm, quad_hbm, gains_ref, lags_hbm, out_ref,
    trace_ref, quad_ref, lags_ref, energy_t, edge_out, edge_in, total, lag_out, lag_group, packed, wide, shifted, picks, acc, part,
    load_sem, total_send, total_recv, edge_send, edge_recv, lag_send, lag_recv, pack_send, pack_recv, fwd_send, fwd_recv,
    part_send, part_recv,
):
    i = lax.axis_index("src")
    j = lax.axis_index("sta")
    stations, block = trace_ref.shape
    cells = lags_ref.shape[1]
    span = STEPS * W // n_src
    rows = span + LAGS
    half = rows // 2
    per = n_src // n_sta
    chips = n_sta // CORES
    everyone = n_src * n_sta
    chip, core = j // CORES, j % CORES
    mate = chip * CORES + (1 - core)

    def remote(src, dst, send, recv, where):
        return pltpu.make_async_remote_copy(
            src_ref=src, dst_ref=dst, send_sem=send, recv_sem=recv,
            device_id=where, device_id_type=pl.DeviceIdType.MESH,
        )

    def wrap(x, n):
        return jnp.where(x >= n, x - n, x)

    def peer(d):
        return wrap(i + d // n_sta, n_src), wrap(j + d % n_sta, n_sta)

    def each(low, high, step):
        for d in range(low, high):
            step(d, 0)

    loads = [
        pltpu.make_async_copy(trace_hbm, trace_ref, load_sem.at[0]),
        pltpu.make_async_copy(quad_hbm, quad_ref, load_sem.at[1]),
        pltpu.make_async_copy(lags_hbm, lags_ref, load_sem.at[2]),
    ]
    for load in loads:
        load.start()
    barrier = pltpu.get_barrier_semaphore()

    def greet(d, carry):
        pl.semaphore_signal(barrier, inc=1, device_id=peer(d), device_id_type=pl.DeviceIdType.MESH)
        return carry

    each(1, everyone, greet)
    for load in loads:
        load.wait()

    lag_out[...] = lags_ref[...].astype(jnp.float32).astype(jnp.bfloat16)
    own_t = (trace_ref[...] * trace_ref[...] + quad_ref[...] * quad_ref[...]).T * gains_ref[...]
    energy_t[LAGS : LAGS + block, :] = own_t
    own_total = jnp.sum(own_t, axis=0, keepdims=True)
    total[i, j] = own_total
    own_mean = own_total / block
    edge_out[0] = (own_t[:LAGS] - own_mean).astype(jnp.bfloat16)
    edge_out[1] = (own_t[block - LAGS :] - own_mean).astype(jnp.bfloat16)
    offset = LAGS - (LAGS // n_src) * i
    upper = energy_t[pl.ds(offset, half), :] - own_mean
    lower = energy_t[pl.ds(offset + half, half), :] - own_mean
    packed[j] = jnp.concatenate([upper, lower], axis=1).astype(jnp.bfloat16)
    pl.semaphore_wait(barrier, everyone - 1)

    def total_copy(d):
        return remote(total.at[i, j], total.at[i, j], total_send.at[d], total_recv.at[d], peer(d))

    pack_copies = [remote(packed.at[j], packed.at[j], pack_send.at[0], pack_recv.at[0], (i, mate))]
    for c in range(1, chips):
        there = wrap(j + c * CORES, n_sta)
        pack_copies.append(remote(packed.at[j], packed.at[j], pack_send.at[c], pack_recv.at[c], (i, there)))
    owner = i // per
    slot = i % per
    lag_copies = [
        remote(lag_out, lag_group.at[j, slot], lag_send.at[d], lag_recv.at[slot * n_sta + j], (wrap(i + d, n_src), owner))
        for d in range(n_src)
    ]
    beside = (wrap(i + n_src - 1, n_src), wrap(i + 1, n_src))
    inside = (i > 0, i < n_src - 1)
    near = list(range(1, 2 * n_sta)) + list(range((n_src - 1) * n_sta, everyone))
    far = range(2 * n_sta, (n_src - 1) * n_sta)
    edge_copies = []
    for d, column in enumerate([j, mate] + [wrap(j + c * CORES, n_sta) for c in range(1, chips)] + [wrap(mate + c * CORES, n_sta) for c in range(1, chips)]):
        edge_copies.append(remote(
            edge_out.at[0], edge_in.at[1, j], edge_send.at[0, d], edge_recv.at[1, j], (wrap(i + n_src - 1, n_src), column)))
        edge_copies.append(remote(
            edge_out.at[1], edge_in.at[0, j], edge_send.at[1, d], edge_recv.at[0, j], (wrap(i + 1, n_src), column)))

    for d in near:
        total_copy(d).start()
    pack_copies[0].start()
    for copy in lag_copies[1:]:
        copy.start()

    @pl.when(owner != j)
    def _():
        lag_copies[0].start()

    @pl.when(owner == j)
    def _():
        lag_group[j, slot] = lag_out[...]

    def send_edges(low, high):
        for side in range(2):

            @pl.when(inside[side])
            def _():
                for copy in edge_copies[low + side : high : 2]:
                    copy.start()

    send_edges(0, 2 * CORES)
    for copy in pack_copies[1:]:
        copy.start()
    send_edges(2 * CORES, 2 * n_sta)

    def send_total(d, carry):
        total_copy(d).start()
        return carry

    for d in far:
        send_total(d, 0)

    for d in near:
        total_copy(d).wait_recv()
    pack_copies[0].wait_recv()

    def take_column(c):
        for side in range(2):
            edge = remote(edge_out.at[side], edge_in.at[side, c], edge_send.at[side, 0], edge_recv.at[side, c], (i, mate))
            pl.when(inside[side])(edge.wait_recv)
        for q in range(per):
            landed = remote(lag_out, lag_group.at[c, q], lag_send.at[0], lag_recv.at[q * n_sta + c], (i, mate))

            @pl.when(jnp.logical_or(j * per + q != i, j != c))
            def _():
                landed.wait_recv()

    low_lanes = lax.broadcasted_iota(jnp.int32, (half, 2 * stations), 1) < stations
    acc[...] = jnp.zeros_like(acc)
    copied = span + LAGS - SUB
    fwd_copies = []
    for phase in range(chips):
        first = ((chip + phase) % chips) * CORES
        if phase >= 1:
            fwd_copies[phase - 1].wait_recv()
        for c in range(CORES):
            take_column(first + c)
        a = packed[first].astype(jnp.float32)
        b = packed[first + 1].astype(jnp.float32)
        wide[pl.ds(offset, half), :] = jnp.where(low_lanes, a, pltpu.roll(b, stations, 1))
        wide[pl.ds(offset + half, half), :] = jnp.where(low_lanes, pltpu.roll(a, stations, 1), b)
        for side, start in ((0, 0), (1, LAGS + block)):
            wide[start : start + LAGS, :] = jnp.concatenate(
                [
                    edge_in[side, first + c].astype(jnp.float32)
                    + (total[beside[side], first + c] - total[i, first + c]) / block
                    for c in range(CORES)
                ],
                axis=1,
            )
        for s in range(SUB):
            shifted[s] = wide[pl.ds(offset + s, copied), :].astype(jnp.bfloat16)
        lag_pair = jnp.concatenate(
            [jnp.concatenate([lag_group[first + c, q] for q in range(per)], axis=1) for c in range(CORES)], axis=0
        )
        if phase == 0:
            for c in range(1, chips):
                source = wrap(j + (chips - c) * CORES, n_sta)
                fwd_copies.append(remote(
                    packed.at[source], packed.at[source], fwd_send.at[c], fwd_recv.at[c], (i, mate)))

        def add_lags(coarse, carry):
            start = pl.multiple_of(coarse * SUB, SUB)
            if phase == 0:

                @pl.when(coarse == LAGS // SUB - 1)
                def _():
                    for c in range(1, chips):
                        pack_copies[c].wait_recv()
                        fwd_copies[c - 1].start()

            for s in range(SUB):
                lag = (start + s).astype(jnp.float32).astype(jnp.bfloat16)
                picks[s * 2 * stations : (s + 1) * 2 * stations, :] = jnp.where(
                    lag_pair == lag, jnp.bfloat16(1), jnp.bfloat16(0)
                )
            left = jnp.concatenate([shifted[s, pl.ds(start, span), :] for s in range(SUB)], axis=1)
            acc[...] += jnp.dot(left, picks[...], preferred_element_type=jnp.float32)
            return carry

        lax.fori_loop(0, LAGS // SUB, add_lags, 0)

    def take_total(d, carry):
        total_copy(d).wait_recv()
        return carry

    for d in far:
        take_total(d, 0)

    def summed(x):
        return jnp.sum(jnp.sum(jnp.sum(x, axis=0), axis=0), axis=1, keepdims=True)

    shift = summed(total[...]) / (block * n_src) - summed(total[pl.ds(i, 1)]) / block
    beam = acc[...] - shift
    part[i, j] = jnp.sum(beam * beam, axis=0, keepdims=True)

    def part_copy(d):
        return remote(part.at[i, j], part.at[i, j], part_send.at[d], part_recv.at[d], peer(d))

    def send_part(d, carry):
        part_copy(d).start()
        return carry

    def take_part(d, carry):
        part_copy(d).wait_recv()
        return carry

    each(1, everyone, send_part)

    for copy in pack_copies + fwd_copies + lag_copies[1:]:
        copy.wait_send()
    for side in range(2):

        @pl.when(inside[side])
        def _():
            for copy in edge_copies[side::2]:
                copy.wait_send()

    @pl.when(owner != j)
    def _():
        lag_copies[0].wait_send()

    def sent(d, carry):
        total_copy(d).wait_send()
        return carry

    each(1, everyone, sent)
    each(1, everyone, take_part)

    share = n_src // STEPS
    place = i % per
    for k in range(STEPS):
        power = jnp.sum(part[k * share : (k + 1) * share], axis=0)
        peak = jnp.max(jnp.max(power, axis=0), axis=1, keepdims=True)
        mine = jnp.sum(part[k * share : (k + 1) * share, owner], axis=0)
        result = mine[:, :cells]
        for q in range(1, per):
            result = jnp.where(place == q, mine[:, q * cells : (q + 1) * cells], result)
        out_ref[k : k + 1, :] = result / peak

    def part_sent(d, carry):
        part_copy(d).wait_send()
        return carry

    each(1, everyone, part_sent)


def on_device(n_src, n_sta, trace, quadrature, gains, lags):
    stations, block = trace.shape
    cells = lags.shape[0]
    per = n_src // n_sta
    chips = n_sta // CORES
    span = STEPS * W // n_src
    rows = span + LAGS
    everyone = n_src * n_sta
    dma = pltpu.SemaphoreType.DMA
    hbm = pl.BlockSpec(memory_space=pltpu.HBM)
    return pl.pallas_call(
        functools.partial(kernel, n_src, n_sta),
        out_shape=jax.ShapeDtypeStruct((STEPS, cells), jnp.float32),
        in_specs=[hbm, hbm, pl.BlockSpec(memory_space=pltpu.VMEM), hbm],
        out_specs=pl.BlockSpec(memory_space=pltpu.VMEM),
        scratch_shapes=[
            pltpu.VMEM((stations, block), jnp.float32),
            pltpu.VMEM((stations, block), jnp.float32),
            pltpu.VMEM((stations, cells), jnp.int32),
            pltpu.VMEM((block + 2 * LAGS, stations), jnp.float32),
            pltpu.VMEM((2, LAGS, stations), jnp.bfloat16),
            pltpu.VMEM((2, n_sta, LAGS, stations), jnp.bfloat16),
            pltpu.VMEM((n_src, n_sta, 1, stations), jnp.float32),
            pltpu.VMEM((stations, cells), jnp.bfloat16),
            pltpu.VMEM((n_sta, per, stations, cells), jnp.bfloat16),
            pltpu.VMEM((n_sta, rows // 2, 2 * stations), jnp.bfloat16),
            pltpu.VMEM((block + 2 * LAGS, 2 * stations), jnp.float32),
            pltpu.VMEM((SUB, rows - SUB, 2 * stations), jnp.bfloat16),
            pltpu.VMEM((SUB * 2 * stations, per * cells), jnp.bfloat16),
            pltpu.VMEM((span, per * cells), jnp.float32),
            pltpu.VMEM((n_src, n_sta, 1, per * cells), jnp.float32),
            dma((3,)),
            dma((everyone,)), dma((everyone,)),
            dma((2, n_sta)), dma((2, n_sta)),
            dma((n_src,)), dma((n_src,)),
            dma((chips,)), dma((chips,)),
            dma((chips,)), dma((chips,)),
            dma((everyone,)), dma((everyone,)),
        ],
        compiler_params=pltpu.CompilerParams(
            collective_id=0, has_side_effects=True, vmem_limit_bytes=62 * 1024 * 1024
        ),
    )(trace, quadrature, gains.reshape(1, stations), lags.T)


def solution(mesh):
    return jax.shard_map(
        functools.partial(on_device, mesh.shape["src"], mesh.shape["sta"]),
        mesh=mesh,
        in_specs=(P("sta", "src"), P("sta", "src"), P("sta"), P("src", "sta")),
        out_specs=P(None, "src"),
        check_vma=False,
    )
```
